128 devices in a mesh: node: 32 (over z, x, core), local: 4 (over y).
Axes of the slice: x: 4, y: 4, z: 4, core: 2. Of those that a mesh axis runs over, the one named last changes fastest.
Arguments:
- tokens: bfloat16 [2048, 4096], P(('node', 'local')), may hold values from -6 to 6
- expert_ids: int32 [2048, 8], P(('node', 'local')), may hold values from 0 to 127, all different within a row; in each aligned block of 16 rows (0 to 15, 16 to 31, ...) at most 2 rows name the same one
- gate_values: float32 [2048, 8], P(('node', 'local')), may hold values from 0.2 to 1
- w_gate: bfloat16 [128, 4096, 1024], P(('node', 'local')), may hold values from -0.09375 to 0.09375
- w_up: bfloat16 [128, 4096, 1024], P(('node', 'local')), may hold values from -0.09375 to 0.09375
- w_down: bfloat16 [128, 1024, 4096], P(('node', 'local')), may hold values from -0.1875 to 0.1875
Outputs:
- combined: bfloat16 [2048, 4096], P(('node', 'local'))
The draws below stay inside these ranges and needn't reach their ends.
Inputs may be any that keep to these rules, and one draw needn't show every extreme that they name: `expert_ids`: each row names 8 different experts. Within the 16 rows of one device no expert is named more than 2 times, and in some device one expert is named exactly 2 times.
All inputs are finite; a program needn't handle non-finite values.
Results may differ from the reference program's by a relative error of at most 0.0057.
Values may be sent and summed in bfloat16 or wider, within the bound.
No kernel may reach another device: no remote copies, remote signals or barrier semaphores. Data moves between devices by JAX's collectives and lax.ppermute only.
A program may use at most 128 MiB of HBM per device.

```python
import math
import jax
import jax.numpy as jnp
import numpy as np
from jax import lax

D = 4096
FF = 1024
TOPK = 8
TOK_DEV = 16
EXPERTS = 128
TOKENS = 2048
CAP = 2


def block_levels(stream_key, extent, pieces, smallest, top_value):
    loudness = 1.0
    for axis_at, blocks in pieces:
        draws = jax.random.uniform(jax.random.fold_in(jax.random.fold_in(stream_key, 6), axis_at), (blocks,), jnp.float32, smallest / len(pieces), top_value / len(pieces))
        loudness = loudness * jnp.repeat(jnp.exp(draws), extent[axis_at] // blocks).reshape((-1,) + (1,) * (len(extent) - 1 - axis_at))
    return loudness


def assign_block(key, own, number, rows, amount, top, reach, skew):
    sequence = jax.random.permutation(key, amount)
    crowded, usual = shares(amount, rows * top, reach, skew, True), shares(amount, rows * top, reach, skew, False)
    places = jnp.arange(amount)

    def named(tallies, offset_by):
        used = int((tallies > 0).sum())
        fixed = max(1, used // 4)
        shifted = fixed + (places - fixed + offset_by * (used - fixed)) % max(1, amount - fixed)
        return jnp.zeros((amount,), jnp.int32).at[sequence[jnp.where(places < fixed, places, shifted)]].set(jnp.asarray(tallies, jnp.int32))

    tallies = jnp.where(number % 4 == 0, named(crowded, number // 4), named(usual, number - number // 4 - 1))
    mixed = jax.random.permutation(jax.random.fold_in(own, 3), amount)
    source_of, taker = mixed[0:amount // 2 * 2:2], mixed[1:amount // 2 * 2:2]
    margin = jnp.minimum(tallies[source_of] - 1, reach - tallies[taker]) // 2
    margin = jnp.where((source_of == sequence[0]) | (taker == sequence[0]) | (tallies[taker] == 0), 0, jnp.maximum(margin, 0))
    shifted = jax.random.randint(jax.random.fold_in(own, 4), (amount // 2,), 0, 1 << 20) % (margin + 1)
    tallies = tallies.at[source_of].add(-shifted).at[taker].add(shifted)
    items = jnp.searchsorted(jnp.cumsum(tallies), jnp.arange(rows * top), side="right").astype(jnp.int32)
    listing = items.reshape(top, rows).T
    listing = listing[jax.random.permutation(jax.random.fold_in(own, 1), rows)]
    offset_by = jax.random.randint(jax.random.fold_in(own, 2), (rows, 1), 0, top)
    return jnp.take_along_axis(listing, (jnp.arange(top)[None, :] + offset_by) % top, axis=1)


def shares(count, total, bound, skew, full):
    portions = [(1 << 20) // math.isqrt(grade ** skew) + 1 for grade in range(1, count + 1)]
    largest = bound if full else min(bound, max(-(-total // count), total * portions[0] // sum(portions)))
    least = 1 if total - largest >= count - 1 else 0
    counts, surplus = [largest] + [least] * (count - 1), total - largest - least * (count - 1)
    while surplus > 0:
        movable = [i for i in range(1, count) if counts[i] < largest] or [i for i in range(1, count) if counts[i] < bound]
        mass, budget = sum([portions[i] for i in movable]), surplus
        for i in movable:
            more = min(bound - counts[i], max(1, budget * portions[i] // mass), surplus)
            counts[i] = counts[i] + more
            surplus = surplus - more
    return np.array(counts)


def centred(rng, dims, scale, reach, shards=(), kind=jnp.bfloat16):
    gain = block_levels(rng, dims, shards, -0.22, 0.18) if shards else 1.0
    values = jax.random.normal(rng, dims, jnp.float32) * scale * gain
    return jnp.minimum(jnp.maximum(values, -reach), reach).astype(kind)


def setup_inputs(seed: int = 0) -> dict:
    key_of = jax.random.split(jax.random.key(seed), 7)
    tokens = centred(key_of[0], (TOKENS, D), 1.0, 6.0, ((0, 128),))
    expert_ids_keys = jax.random.split(jax.random.fold_in(key_of[1], 1), TOKENS // TOK_DEV)
    expert_ids_turns = jax.random.permutation(jax.random.fold_in(key_of[1], 3), TOKENS // TOK_DEV)
    expert_ids = jax.vmap(lambda own, number: assign_block(jax.random.fold_in(key_of[1], 2), own, number, TOK_DEV, EXPERTS, TOPK, CAP, 2))(expert_ids_keys, expert_ids_turns).reshape((TOKENS, TOPK))
    gate_values = jnp.clip(0.2 + 0.8 * jax.random.uniform(key_of[2], (TOKENS, TOPK), jnp.float32) ** block_levels(key_of[2], (TOKENS, TOPK), ((0, 128),), -0.2, 0.2), 0.2, 1.0)
    w_gate = centred(key_of[3], (EXPERTS, D, FF), D ** -0.5, 0.09375, ((0, 128),))
    w_up = centred(key_of[4], (EXPERTS, D, FF), D ** -0.5, 0.09375, ((0, 128),))
    w_down = centred(key_of[5], (EXPERTS, FF, D), FF ** -0.5, 0.1875, ((0, 128),))
    return {"tokens": tokens, "expert_ids": expert_ids, "gate_values": gate_values, "w_gate": w_gate, "w_up": w_up, "w_down": w_down}


def expert(operands):
    rows, gate_proj, up_proj, down_proj = operands
    gate_part = jnp.dot(rows, gate_proj, preferred_element_type=jnp.float32)
    up_part = jnp.dot(rows, up_proj, preferred_element_type=jnp.float32)
    hidden = (jax.nn.silu(gate_part) * up_part).astype(jnp.bfloat16)
    return jnp.dot(hidden, down_proj, preferred_element_type=jnp.float32).astype(jnp.bfloat16)


def reference(tokens, expert_ids, gate_values, w_gate, w_up, w_down):
    block_count = TOKENS // TOK_DEV
    pair_count = TOK_DEV * TOPK
    flat_ids = expert_ids.reshape(block_count, pair_count).astype(jnp.int32)
    labels = jnp.arange(EXPERTS, dtype=jnp.int32)
    onehot = (flat_ids[:, :, None] == labels[None, None, :]).astype(jnp.int32)
    before = jnp.cumsum(onehot, axis=1) - onehot
    slot_index = jnp.sum(before * onehot, axis=2).astype(jnp.int32)
    block_start = (jnp.arange(block_count, dtype=jnp.int32) * CAP)[:, None]
    position = (flat_ids * (block_count * CAP) + block_start + slot_index).reshape(-1)
    pair_rows = jnp.repeat(tokens.reshape(block_count, TOK_DEV, D), TOPK, axis=1).reshape(-1, D)
    buffer = jnp.zeros((EXPERTS * block_count * CAP, D), jnp.bfloat16).at[position].set(pair_rows)
    buffer = buffer.reshape(EXPERTS, block_count * CAP, D)
    expert_out = lax.map(expert, (buffer, w_gate, w_up, w_down))
    picked = expert_out.reshape(-1, D)[position].reshape(TOKENS, TOPK, D)
    combined = jnp.sum(picked.astype(jnp.float32) * gate_values[:, :, None], axis=1)
    return combined.astype(jnp.bfloat16)
```

```python
import functools

import jax
import jax.numpy as jnp
from jax import lax
from jax.experimental import pallas as pl
from jax.experimental.pallas import tpu as pltpu
from jax.sharding import PartitionSpec as P

CAP = 2
PARTS = 4
ROWS = CAP * PARTS
BF16 = jnp.bfloat16
F32 = jnp.float32


def vmem(count):
    return [pl.BlockSpec(memory_space=pltpu.VMEM)] * count


def routing(ids_t, experts):
    top, toks = ids_t.shape
    shape = (experts * ROWS, PARTS * toks)
    row = lax.broadcasted_iota(jnp.int32, shape, 0)
    col = lax.broadcasted_iota(jnp.int32, shape, 1)
    wide = jnp.concatenate([ids_t] * PARTS, axis=1)
    named = [(row // ROWS) == wide[k : k + 1, :] for k in range(top)]
    member = functools.reduce(jnp.logical_or, named).astype(F32)
    square = (PARTS * toks, PARTS * toks)
    first = lax.broadcasted_iota(jnp.int32, square, 0)
    second = lax.broadcasted_iota(jnp.int32, square, 1)
    earlier = ((first // toks == second // toks) & (first < second)).astype(F32)
    before = jnp.dot(member.astype(BF16), earlier.astype(BF16), preferred_element_type=F32)
    slot = ((row // PARTS) % CAP).astype(F32)
    own = (before == slot) & (row % PARTS == col // toks)
    return named, member, own


def dispatch_kernel(ids_ref, tok_ref, out_ref, tok_parts, select):
    toks = tok_ref.shape[0]
    wide = tok_parts.shape[1]
    experts = out_ref.shape[0] // ROWS
    for part in range(PARTS):
        tok_parts[part * toks : (part + 1) * toks, :] = tok_ref[:, part * wide : (part + 1) * wide]
    _, member, own = routing(ids_ref[...], experts)
    select[...] = jnp.where(own, member, 0.0).astype(BF16)
    step = 256

    @pl.loop(0, out_ref.shape[0] // step)
    def _(i):
        rows = pl.ds(pl.multiple_of(i * step, step), step)
        out_ref[rows, :] = jnp.dot(select[rows, :], tok_parts[...], preferred_element_type=F32).astype(BF16)


def weights_kernel(ids_ref, gates_ref, out_ref):
    lanes = out_ref.shape[1] // 3
    experts = out_ref.shape[0] // ROWS
    named, _, own = routing(ids_ref[...], experts)
    gates = jnp.concatenate([gates_ref[...]] * PARTS, axis=1)
    total = jnp.zeros(own.shape, F32)
    for k, here in enumerate(named):
        total = total + jnp.where(here, gates[k : k + 1, :], 0.0)
    rest = jnp.where(own, total, 0.0)
    for term in range(3):
        piece = rest.astype(BF16)
        out_ref[:, term * lanes : (term + 1) * lanes] = piece
        rest = rest - piece.astype(F32)


def combine_kernel(weights_ref, rows_ref, out_ref):
    toks = out_ref.shape[0]
    wide = rows_ref.shape[1]
    lanes = weights_ref.shape[1] // 3
    terms = lax.dot_general(
        weights_ref[...], rows_ref[...], (((0,), (0,)), ((), ())), preferred_element_type=F32
    )
    total = terms[:lanes] + terms[lanes : 2 * lanes] + terms[2 * lanes :]
    for part in range(PARTS):
        out_ref[:, part * wide : (part + 1) * wide] = total[part * toks : (part + 1) * toks].astype(BF16)


def expert_kernel(rows_ref, gate_hbm, up_hbm, down_hbm, out_ref, gate, up, down, x, hidden, sems):
    wide = rows_ref.shape[1]
    depth, units = gate.shape
    count = x.shape[0]
    chunk = 256
    pieces = 256 // ROWS
    loads = []
    for i in range(units // chunk):
        cols = pl.ds(i * chunk, chunk)
        loads.append(
            (
                pltpu.make_async_copy(gate_hbm.at[:, cols], gate.at[:, cols], sems.at[0, i]),
                pltpu.make_async_copy(up_hbm.at[:, cols], up.at[:, cols], sems.at[1, i]),
            )
        )
    down_loads = []
    for part in range(PARTS):
        cols = pl.ds(part * wide, wide)
        down_loads.append(pltpu.make_async_copy(down_hbm.at[:, cols], down.at[:, cols], sems.at[2, part]))
    for pair in loads:
        pair[0].start()
        pair[1].start()
    for load in down_loads:
        load.start()
    first = lax.broadcasted_iota(jnp.int32, (256, 256), 0)
    second = lax.broadcasted_iota(jnp.int32, (256, 256), 1)
    ungroup = (second == (first % pieces) * ROWS + first // pieces).astype(F32).astype(BF16)
    group = (first == (second % pieces) * ROWS + second // pieces).astype(F32).astype(BF16)
    half = count // CAP
    for b in range(rows_ref.shape[0] // 256):
        spread = jnp.dot(ungroup, rows_ref[b * 256 : (b + 1) * 256, :], preferred_element_type=F32).astype(BF16)
        for r in range(ROWS):
            slot, part = r // PARTS, r % PARTS
            start = slot * half + b * pieces
            x[start : start + pieces, part * wide : (part + 1) * wide] = spread[r * pieces : (r + 1) * pieces]
    for i in range(units // chunk):
        loads[i][0].wait()
        g = jnp.dot(x[...], gate[:, i * chunk : (i + 1) * chunk], preferred_element_type=F32)
        loads[i][1].wait()
        u = jnp.dot(x[...], up[:, i * chunk : (i + 1) * chunk], preferred_element_type=F32)
        hidden[:, i * chunk : (i + 1) * chunk] = (g / (1.0 + jnp.exp(-g)) * u).astype(BF16)
    for part in range(PARTS):
        down_loads[part].wait()
        y = jnp.dot(hidden[...], down[:, part * wide : (part + 1) * wide], preferred_element_type=F32)
        x[:, part * wide : (part + 1) * wide] = y.astype(BF16)
    for b in range(rows_ref.shape[0] // 256):
        parts = []
        for r in range(ROWS):
            slot, part = r // PARTS, r % PARTS
            start = slot * half + b * pieces
            parts.append(x[start : start + pieces, part * wide : (part + 1) * wide])
        out_ref[b * 256 : (b + 1) * 256, :] = jnp.dot(
            group, jnp.concatenate(parts, axis=0), preferred_element_type=F32
        ).astype(BF16)


def on_device(tokens, expert_ids, gate_values, w_gate, w_up, w_down):
    experts = lax.axis_size("node") * lax.axis_size("local")
    toks, features = tokens.shape
    units = w_gate.shape[2]
    wide = features // PARTS
    lanes = PARTS * toks
    piece_rows = experts * ROWS
    ids_t, gates_t = expert_ids.T, gate_values.T
    slots = jax.ShapeDtypeStruct((piece_rows, wide), BF16)

    def exchange(rows):
        moved = lax.all_to_all(
            rows.reshape(experts, ROWS, wide), ("node", "local"), split_axis=0, concat_axis=0, tiled=True
        )
        return moved.reshape(piece_rows, wide)

    outgoing = pl.pallas_call(
        dispatch_kernel,
        out_shape=slots,
        in_specs=vmem(2),
        out_specs=pl.BlockSpec(memory_space=pltpu.VMEM),
        scratch_shapes=[pltpu.VMEM((lanes, wide), BF16), pltpu.VMEM((piece_rows, lanes), BF16)],
        compiler_params=pltpu.CompilerParams(vmem_limit_bytes=16 << 20),
        name="dispatch",
    )(ids_t, tokens)
    weights = pl.pallas_call(
        weights_kernel,
        out_shape=jax.ShapeDtypeStruct((piece_rows, 3 * lanes), BF16),
        in_specs=vmem(2),
        out_specs=pl.BlockSpec(memory_space=pltpu.VMEM),
        compiler_params=pltpu.CompilerParams(vmem_limit_bytes=16 << 20),
        cost_estimate=pl.CostEstimate(flops=10_000_000, bytes_accessed=1_000_000, transcendentals=0),
        name="weights",
    )(ids_t, gates_t)
    finished = pl.pallas_call(
        expert_kernel,
        out_shape=slots,
        in_specs=vmem(1) + [pl.BlockSpec(memory_space=pl.ANY)] * 3,
        out_specs=pl.BlockSpec(memory_space=pltpu.VMEM),
        scratch_shapes=[
            pltpu.VMEM((features, units), BF16),
            pltpu.VMEM((features, units), BF16),
            pltpu.VMEM((units, features), BF16),
            pltpu.VMEM((experts * CAP, features), BF16),
            pltpu.VMEM((experts * CAP, units), BF16),
            pltpu.SemaphoreType.DMA((3, 4)),
        ],
        compiler_params=pltpu.CompilerParams(vmem_limit_bytes=44 << 20),
        name="expert",
    )(exchange(outgoing), w_gate[0], w_up[0], w_down[0])
    return pl.pallas_call(
        combine_kernel,
        out_shape=jax.ShapeDtypeStruct((toks, features), BF16),
        in_specs=vmem(2),
        out_specs=pl.BlockSpec(memory_space=pltpu.VMEM),
        compiler_params=pltpu.CompilerParams(vmem_limit_bytes=16 << 20),
        name="combine",
    )(weights, exchange(finished))


def solution(mesh):
    rows = P(("node", "local"), None)
    block = P(("node", "local"), None, None)
    return jax.shard_map(
        on_device,
        mesh=mesh,
        in_specs=(rows, rows, rows, block, block, block),
        out_specs=rows,
        check_vma=False,
    )
```

```python
import functools

import jax
import jax.numpy as jnp
from jax import lax
from jax.experimental import pallas as pl
from jax.experimental.pallas import tpu as pltpu
from jax.sharding import PartitionSpec as P

CAP = 2
PARTS = 4
ROWS = CAP * PARTS
BF16 = jnp.bfloat16
F32 = jnp.float32


def vmem(count):
    return [pl.BlockSpec(memory_space=pltpu.VMEM)] * count


def routing(ids_t, experts):
    top, toks = ids_t.shape
    shape = (experts * ROWS, PARTS * toks)
    row = lax.broadcasted_iota(jnp.int32, shape, 0)
    col = lax.broadcasted_iota(jnp.int32, shape, 1)
    wide = jnp.concatenate([ids_t] * PARTS, axis=1)
    named = [(row // ROWS) == wide[k : k + 1, :] for k in range(top)]
    member = functools.reduce(jnp.logical_or, named).astype(F32)
    square = (PARTS * toks, PARTS * toks)
    first = lax.broadcasted_iota(jnp.int32, square, 0)
    second = lax.broadcasted_iota(jnp.int32, square, 1)
    earlier = ((first // toks == second // toks) & (first < second)).astype(F32)
    before = jnp.dot(member.astype(BF16), earlier.astype(BF16), preferred_element_type=F32)
    slot = ((row // PARTS) % CAP).astype(F32)
    own = (before == slot) & (row % PARTS == col // toks)
    return named, member, own


def dispatch_kernel(ids_ref, tok_ref, out_ref, tok_parts, select):
    toks = tok_ref.shape[0]
    wide = tok_parts.shape[1]
    experts = out_ref.shape[0] // ROWS
    for part in range(PARTS):
        tok_parts[part * toks : (part + 1) * toks, :] = tok_ref[:, part * wide : (part + 1) * wide]
    _, member, own = routing(ids_ref[...], experts)
    select[...] = jnp.where(own, member, 0.0).astype(BF16)
    step = 256

    @pl.loop(0, out_ref.shape[0] // step)
    def _(i):
        rows = pl.ds(pl.multiple_of(i * step, step), step)
        out_ref[rows, :] = jnp.dot(select[rows, :], tok_parts[...], preferred_element_type=F32).astype(BF16)


def weights_kernel(ids_ref, gates_ref, out_ref):
    lanes = out_ref.shape[1] // 3
    experts = out_ref.shape[0] // ROWS
    named, _, own = routing(ids_ref[...], experts)
    gates = jnp.concatenate([gates_ref[...]] * PARTS, axis=1)
    total = jnp.zeros(own.shape, F32)
    for k, here in enumerate(named):
        total = total + jnp.where(here, gates[k : k + 1, :], 0.0)
    rest = jnp.where(own, total, 0.0)
    for term in range(3):
        piece = rest.astype(BF16)
        out_ref[:, term * lanes : (term + 1) * lanes] = piece
        rest = rest - piece.astype(F32)


def combine_kernel(weights_ref, rows_ref, out_ref):
    toks = out_ref.shape[0]
    wide = rows_ref.shape[1]
    lanes = weights_ref.shape[1] // 3
    terms = lax.dot_general(
        weights_ref[...], rows_ref[...], (((0,), (0,)), ((), ())), preferred_element_type=F32
    )
    total = terms[:lanes] + terms[lanes : 2 * lanes] + terms[2 * lanes :]
    for part in range(PARTS):
        out_ref[:, part * wide : (part + 1) * wide] = total[part * toks : (part + 1) * toks].astype(BF16)


def expert_kernel(rows_ref, gate_ref, up_ref, down_ref, out_ref, x, hidden):
    wide = rows_ref.shape[1]
    units = gate_ref.shape[1]
    count = x.shape[0]
    chunk = 256
    pieces = 256 // ROWS
    first = lax.broadcasted_iota(jnp.int32, (256, 256), 0)
    second = lax.broadcasted_iota(jnp.int32, (256, 256), 1)
    ungroup = (second == (first % pieces) * ROWS + first // pieces).astype(F32).astype(BF16)
    group = (first == (second % pieces) * ROWS + second // pieces).astype(F32).astype(BF16)
    half = count // CAP
    for b in range(rows_ref.shape[0] // 256):
        spread = jnp.dot(ungroup, rows_ref[b * 256 : (b + 1) * 256, :], preferred_element_type=F32).astype(BF16)
        for r in range(ROWS):
            slot, part = r // PARTS, r % PARTS
            start = slot * half + b * pieces
            x[start : start + pieces, part * wide : (part + 1) * wide] = spread[r * pieces : (r + 1) * pieces]
    for i in range(units // chunk):
        cols = slice(i * chunk, (i + 1) * chunk)
        g = jnp.dot(x[...], gate_ref[:, cols], preferred_element_type=F32)
        u = jnp.dot(x[...], up_ref[:, cols], preferred_element_type=F32)
        hidden[:, cols] = (g / (1.0 + jnp.exp(-g)) * u).astype(BF16)
    for part in range(PARTS):
        cols = slice(part * wide, (part + 1) * wide)
        x[:, cols] = jnp.dot(hidden[...], down_ref[:, cols], preferred_element_type=F32).astype(BF16)
    for b in range(rows_ref.shape[0] // 256):
        parts = []
        for r in range(ROWS):
            slot, part = r // PARTS, r % PARTS
            start = slot * half + b * pieces
            parts.append(x[start : start + pieces, part * wide : (part + 1) * wide])
        out_ref[b * 256 : (b + 1) * 256, :] = jnp.dot(
            group, jnp.concatenate(parts, axis=0), preferred_element_type=F32
        ).astype(BF16)


def on_device(tokens, expert_ids, gate_values, w_gate, w_up, w_down):
    experts = lax.axis_size("node") * lax.axis_size("local")
    toks, features = tokens.shape
    units = w_gate.shape[2]
    wide = features // PARTS
    lanes = PARTS * toks
    piece_rows = experts * ROWS
    ids_t, gates_t = expert_ids.T, gate_values.T
    slots = jax.ShapeDtypeStruct((piece_rows, wide), BF16)

    def exchange(rows):
        moved = lax.all_to_all(
            rows.reshape(experts, ROWS, wide), ("node", "local"), split_axis=0, concat_axis=0, tiled=True
        )
        return moved.reshape(piece_rows, wide)

    outgoing = pl.pallas_call(
        dispatch_kernel,
        out_shape=slots,
        in_specs=vmem(2),
        out_specs=pl.BlockSpec(memory_space=pltpu.VMEM),
        scratch_shapes=[pltpu.VMEM((lanes, wide), BF16), pltpu.VMEM((piece_rows, lanes), BF16)],
        compiler_params=pltpu.CompilerParams(vmem_limit_bytes=16 << 20),
        cost_estimate=pl.CostEstimate(flops=20_000_000_000, bytes_accessed=100_000_000, transcendentals=0),
        name="dispatch",
    )(ids_t, tokens)
    weights = pl.pallas_call(
        weights_kernel,
        out_shape=jax.ShapeDtypeStruct((piece_rows, 3 * lanes), BF16),
        in_specs=vmem(2),
        out_specs=pl.BlockSpec(memory_space=pltpu.VMEM),
        compiler_params=pltpu.CompilerParams(vmem_limit_bytes=16 << 20),
        cost_estimate=pl.CostEstimate(flops=10_000_000, bytes_accessed=1_000_000, transcendentals=0),
        name="weights",
    )(ids_t, gates_t)
    finished = pl.pallas_call(
        expert_kernel,
        out_shape=slots,
        in_specs=vmem(4),
        out_specs=pl.BlockSpec(memory_space=pltpu.VMEM),
        scratch_shapes=[
            pltpu.VMEM((experts * CAP, features), BF16),
            pltpu.VMEM((experts * CAP, units), BF16),
        ],
        compiler_params=pltpu.CompilerParams(vmem_limit_bytes=16 << 20),
        cost_estimate=pl.CostEstimate(flops=6_500_000_000, bytes_accessed=30_000_000, transcendentals=0),
        name="expert",
    )(exchange(outgoing), w_gate[0], w_up[0], w_down[0])
    return pl.pallas_call(
        combine_kernel,
        out_shape=jax.ShapeDtypeStruct((toks, features), BF16),
        in_specs=vmem(2),
        out_specs=pl.BlockSpec(memory_space=pltpu.VMEM),
        compiler_params=pltpu.CompilerParams(vmem_limit_bytes=16 << 20),
        name="combine",
    )(weights, exchange(finished))


def solution(mesh):
    rows = P(("node", "local"), None)
    block = P(("node", "local"), None, None)
    return jax.shard_map(
        on_device,
        mesh=mesh,
        in_specs=(rows, rows, rows, block, block, block),
        out_specs=rows,
        check_vma=False,
    )
```

```python
import functools

import jax
import jax.numpy as jnp
from jax import lax
from jax.experimental import pallas as pl
from jax.experimental.pallas import tpu as pltpu
from jax.sharding import PartitionSpec as P

CAP = 2
PARTS = 4
ROWS = CAP * PARTS
BF16 = jnp.bfloat16
F32 = jnp.float32


def vmem(count):
    return [pl.BlockSpec(memory_space=pltpu.VMEM)] * count


def lane_columns(wide_t):
    top, toks = wide_t.shape
    return jnp.concatenate([wide_t] * (128 // toks), axis=1).T[: PARTS * toks]


def routing(ids_t, values_t, experts):
    top, toks = ids_t.shape
    shape = (PARTS * toks, experts * ROWS)
    lane = lax.broadcasted_iota(jnp.int32, shape, 0)
    row = lax.broadcasted_iota(jnp.int32, shape, 1)
    ids = lane_columns(ids_t)
    expert = row // ROWS
    named = [expert == ids[:, k : k + 1] for k in range(top)]
    member = functools.reduce(jnp.logical_or, named).astype(F32)
    square = (PARTS * toks, PARTS * toks)
    later = lax.broadcasted_iota(jnp.int32, square, 0)
    sooner = lax.broadcasted_iota(jnp.int32, square, 1)
    earlier = ((later // toks == sooner // toks) & (sooner < later)).astype(F32).astype(BF16)
    before = jnp.dot(earlier, member.astype(BF16), preferred_element_type=F32)
    slot = ((row // PARTS) % CAP).astype(F32)
    own = (before == slot) & (row % PARTS == lane // toks)
    if values_t is not None:
        values = lane_columns(values_t)
        member = jnp.zeros(shape, F32)
        for k, here in enumerate(named):
            member = jnp.where(here, values[:, k : k + 1], member)
    return jnp.where(own, member, 0.0)


def dispatch_kernel(ids_hbm, tok_hbm, out_ref, ids_ref, tok_parts, sems):
    toks = tok_hbm.shape[0]
    wide = tok_parts.shape[1]
    experts = out_ref.shape[0] // ROWS
    ids_load = pltpu.make_async_copy(ids_hbm, ids_ref, sems.at[PARTS])
    ids_load.start()
    loads = []
    for part in range(PARTS):
        source = tok_hbm.at[:, pl.ds(part * wide, wide)]
        loads.append(pltpu.make_async_copy(source, tok_parts.at[pl.ds(part * toks, toks), :], sems.at[part]))
        loads[-1].start()
    ids_load.wait()
    select = routing(ids_ref[...], None, experts).astype(BF16)
    for load in loads:
        load.wait()
    out_ref[...] = lax.dot_general(
        select, tok_parts[...], (((0,), (0,)), ((), ())), preferred_element_type=F32
    ).astype(BF16)


def combine_weights(ids_t, gates_t, out_ref):
    lanes = out_ref.shape[0] // 3
    rest = routing(ids_t, gates_t, out_ref.shape[1] // ROWS)
    for term in range(3):
        piece = rest.astype(BF16)
        out_ref[term * lanes : (term + 1) * lanes, :] = piece
        rest = rest - piece.astype(F32)


def combine_kernel(weights_ref, rows_ref, out_ref):
    toks = out_ref.shape[0]
    wide = rows_ref.shape[1]
    lanes = weights_ref.shape[0] // 3
    terms = jnp.dot(weights_ref[...], rows_ref[...], preferred_element_type=F32)
    total = terms[:lanes] + terms[lanes : 2 * lanes] + terms[2 * lanes :]
    for part in range(PARTS):
        out_ref[:, part * wide : (part + 1) * wide] = total[part * toks : (part + 1) * toks].astype(BF16)


def expert_kernel(ids_ref, gates_ref, rows_ref, gate_ref, up_ref, down_ref, out_ref, weights_ref, x, hidden):
    wide = rows_ref.shape[1]
    units = gate_ref.shape[1]
    count = x.shape[0]
    chunk = 256
    pieces = 256 // ROWS
    first = lax.broadcasted_iota(jnp.int32, (256, 256), 0)
    second = lax.broadcasted_iota(jnp.int32, (256, 256), 1)
    ungroup = (second == (first % pieces) * ROWS + first // pieces).astype(F32).astype(BF16)
    group = (first == (second % pieces) * ROWS + second // pieces).astype(F32).astype(BF16)
    half = count // CAP
    for b in range(rows_ref.shape[0] // 256):
        spread = jnp.dot(ungroup, rows_ref[b * 256 : (b + 1) * 256, :], preferred_element_type=F32).astype(BF16)
        for r in range(ROWS):
            slot, part = r // PARTS, r % PARTS
            start = slot * half + b * pieces
            x[start : start + pieces, part * wide : (part + 1) * wide] = spread[r * pieces : (r + 1) * pieces]
    for i in range(units // chunk):
        cols = slice(i * chunk, (i + 1) * chunk)
        g = jnp.dot(x[...], gate_ref[:, cols], preferred_element_type=F32)
        u = jnp.dot(x[...], up_ref[:, cols], preferred_element_type=F32)
        hidden[:, cols] = (g / (1.0 + jnp.exp(-g)) * u).astype(BF16)
        if i == 0:
            combine_weights(ids_ref[...], gates_ref[...], weights_ref)
    for part in range(PARTS):
        cols = slice(part * wide, (part + 1) * wide)
        x[:, cols] = jnp.dot(hidden[...], down_ref[:, cols], preferred_element_type=F32).astype(BF16)
    for b in range(rows_ref.shape[0] // 256):
        parts = []
        for r in range(ROWS):
            slot, part = r // PARTS, r % PARTS
            start = slot * half + b * pieces
            parts.append(x[start : start + pieces, part * wide : (part + 1) * wide])
        out_ref[b * 256 : (b + 1) * 256, :] = jnp.dot(
            group, jnp.concatenate(parts, axis=0), preferred_element_type=F32
        ).astype(BF16)


def on_device(tokens, expert_ids, gate_values, w_gate, w_up, w_down):
    experts = lax.axis_size("node") * lax.axis_size("local")
    toks, features = tokens.shape
    units = w_gate.shape[2]
    wide = features // PARTS
    lanes = PARTS * toks
    piece_rows = experts * ROWS
    ids_t, gates_t = expert_ids.T, gate_values.T
    slots = jax.ShapeDtypeStruct((piece_rows, wide), BF16)

    def exchange(rows):
        moved = lax.all_to_all(
            rows.reshape(experts, ROWS, wide), ("node", "local"), split_axis=0, concat_axis=0, tiled=True
        )
        return moved.reshape(piece_rows, wide)

    outgoing = pl.pallas_call(
        dispatch_kernel,
        out_shape=slots,
        in_specs=[pl.BlockSpec(memory_space=pltpu.HBM)] * 2,
        out_specs=pl.BlockSpec(memory_space=pltpu.VMEM),
        scratch_shapes=[
            pltpu.VMEM(ids_t.shape, jnp.int32),
            pltpu.VMEM((lanes, wide), BF16),
            pltpu.SemaphoreType.DMA((PARTS + 1,)),
        ],
        compiler_params=pltpu.CompilerParams(vmem_limit_bytes=16 << 20),
        cost_estimate=pl.CostEstimate(flops=20_000_000_000, bytes_accessed=100_000_000, transcendentals=0),
        name="dispatch",
    )(pltpu.with_memory_space_constraint(ids_t, pltpu.HBM), pltpu.with_memory_space_constraint(tokens, pltpu.HBM))
    finished, weights = pl.pallas_call(
        expert_kernel,
        out_shape=[slots, jax.ShapeDtypeStruct((3 * lanes, piece_rows), BF16)],
        in_specs=vmem(6),
        out_specs=vmem(2),
        scratch_shapes=[
            pltpu.VMEM((experts * CAP, features), BF16),
            pltpu.VMEM((experts * CAP, units), BF16),
        ],
        compiler_params=pltpu.CompilerParams(vmem_limit_bytes=16 << 20),
        cost_estimate=pl.CostEstimate(flops=6_500_000_000, bytes_accessed=30_000_000, transcendentals=0),
        name="expert",
    )(ids_t, gates_t, exchange(outgoing), w_gate[0], w_up[0], w_down[0])
    return pl.pallas_call(
        combine_kernel,
        out_shape=jax.ShapeDtypeStruct((toks, features), BF16),
        in_specs=vmem(2),
        out_specs=pl.BlockSpec(memory_space=pltpu.VMEM),
        compiler_params=pltpu.CompilerParams(vmem_limit_bytes=16 << 20),
        name="combine",
    )(weights, exchange(finished))


def solution(mesh):
    rows = P(("node", "local"), None)
    block = P(("node", "local"), None, None)
    return jax.shard_map(
        on_device,
        mesh=mesh,
        in_specs=(rows, rows, rows, block, block, block),
        out_specs=rows,
        check_vma=False,
    )
```

```python
import functools

import jax
import jax.numpy as jnp
from jax import lax
from jax.experimental import pallas as pl
from jax.experimental.pallas import tpu as pltpu
from jax.sharding import PartitionSpec as P

CAP = 2
PARTS = 4
ROWS = CAP * PARTS
BF16 = jnp.bfloat16
F32 = jnp.float32


def vmem(count):
    return [pl.BlockSpec(memory_space=pltpu.VMEM)] * count


def columns(wide_t):
    top, toks = wide_t.shape
    return jnp.concatenate([wide_t] * (128 // toks), axis=1).T[:toks]


def routing(ids_t, values_t, experts):
    top, toks = ids_t.shape
    shape = (toks, experts * ROWS)
    row = lax.broadcasted_iota(jnp.int32, shape, 1)
    ids = columns(ids_t)
    expert = row // ROWS
    named = [expert == ids[:, k : k + 1] for k in range(top)]
    member = functools.reduce(jnp.logical_or, named).astype(F32)
    later = lax.broadcasted_iota(jnp.int32, (toks, toks), 0)
    sooner = lax.broadcasted_iota(jnp.int32, (toks, toks), 1)
    earlier = (sooner < later).astype(F32).astype(BF16)
    before = jnp.dot(earlier, member.astype(BF16), preferred_element_type=F32)
    own = before == ((row // PARTS) % CAP).astype(F32)
    if values_t is not None:
        values = columns(values_t)
        member = jnp.zeros(shape, F32)
        for k, here in enumerate(named):
            member = jnp.where(here, values[:, k : k + 1], member)
    return jnp.where(own, member, 0.0)


def by_part(filled):
    part_of = lax.broadcasted_iota(jnp.int32, filled.shape, 1) % PARTS
    return jnp.concatenate([jnp.where(part_of == part, filled, 0.0) for part in range(PARTS)], axis=0).astype(BF16)


def dispatch_kernel(ids_hbm, tok_hbm, out_ref, ids_ref, tok_parts, sems):
    toks = tok_hbm.shape[0]
    wide = tok_parts.shape[1]
    experts = out_ref.shape[0] // ROWS
    ids_load = pltpu.make_async_copy(ids_hbm, ids_ref, sems.at[PARTS])
    ids_load.start()
    loads = []
    for part in range(PARTS):
        source = tok_hbm.at[:, pl.ds(part * wide, wide)]
        loads.append(pltpu.make_async_copy(source, tok_parts.at[pl.ds(part * toks, toks), :], sems.at[part]))
        loads[-1].start()
    ids_load.wait()
    select = by_part(routing(ids_ref[...], None, experts))
    for load in loads:
        load.wait()
    out_ref[...] = lax.dot_general(
        select, tok_parts[...], (((0,), (0,)), ((), ())), preferred_element_type=F32
    ).astype(BF16)


def combine_weights(ids_t, gates_t, out_ref):
    lanes = out_ref.shape[0] // 3
    rest = routing(ids_t, gates_t, out_ref.shape[1] // ROWS)
    for term in range(3):
        piece = rest.astype(BF16).astype(F32)
        out_ref[term * lanes : (term + 1) * lanes, :] = by_part(piece)
        rest = rest - piece


def combine_kernel(weights_ref, rows_ref, out_ref):
    toks = out_ref.shape[0]
    wide = rows_ref.shape[1]
    lanes = weights_ref.shape[0] // 3
    terms = jnp.dot(weights_ref[...], rows_ref[...], preferred_element_type=F32)
    total = terms[:lanes] + terms[lanes : 2 * lanes] + terms[2 * lanes :]
    for part in range(PARTS):
        out_ref[:, part * wide : (part + 1) * wide] = total[part * toks : (part + 1) * toks].astype(BF16)


def expert_kernel(ids_ref, gates_ref, rows_ref, gate_ref, up_ref, down_ref, out_ref, weights_ref, x, hidden):
    wide = rows_ref.shape[1]
    units = gate_ref.shape[1]
    count = x.shape[0]
    chunk = 256
    pieces = 256 // ROWS
    first = lax.broadcasted_iota(jnp.int32, (256, 256), 0)
    second = lax.broadcasted_iota(jnp.int32, (256, 256), 1)
    ungroup = (second == (first % pieces) * ROWS + first // pieces).astype(F32).astype(BF16)
    group = (first == (second % pieces) * ROWS + second // pieces).astype(F32).astype(BF16)
    half = count // CAP
    for b in range(rows_ref.shape[0] // 256):
        spread = jnp.dot(ungroup, rows_ref[b * 256 : (b + 1) * 256, :], preferred_element_type=F32).astype(BF16)
        for r in range(ROWS):
            slot, part = r // PARTS, r % PARTS
            start = slot * half + b * pieces
            x[start : start + pieces, part * wide : (part + 1) * wide] = spread[r * pieces : (r + 1) * pieces]
    for i in range(units // chunk):
        cols = slice(i * chunk, (i + 1) * chunk)
        g = jnp.dot(x[...], gate_ref[:, cols], preferred_element_type=F32)
        u = jnp.dot(x[...], up_ref[:, cols], preferred_element_type=F32)
        hidden[:, cols] = (g / (1.0 + jnp.exp(-g)) * u).astype(BF16)
        if i == 0:
            combine_weights(ids_ref[...], gates_ref[...], weights_ref)
    for part in range(PARTS):
        cols = slice(part * wide, (part + 1) * wide)
        x[:, cols] = jnp.dot(hidden[...], down_ref[:, cols], preferred_element_type=F32).astype(BF16)
    for b in range(rows_ref.shape[0] // 256):
        parts = []
        for r in range(ROWS):
            slot, part = r // PARTS, r % PARTS
            start = slot * half + b * pieces
            parts.append(x[start : start + pieces, part * wide : (part + 1) * wide])
        out_ref[b * 256 : (b + 1) * 256, :] = jnp.dot(
            group, jnp.concatenate(parts, axis=0), preferred_element_type=F32
        ).astype(BF16)


def on_device(tokens, expert_ids, gate_values, w_gate, w_up, w_down):
    experts = lax.axis_size("node") * lax.axis_size("local")
    toks, features = tokens.shape
    units = w_gate.shape[2]
    wide = features // PARTS
    lanes = PARTS * toks
    piece_rows = experts * ROWS
    ids_t, gates_t = expert_ids.T, gate_values.T
    slots = jax.ShapeDtypeStruct((piece_rows, wide), BF16)

    def exchange(rows):
        moved = lax.all_to_all(
            rows.reshape(experts, ROWS, wide), ("node", "local"), split_axis=0, concat_axis=0, tiled=True
        )
        return moved.reshape(piece_rows, wide)

    outgoing = pl.pallas_call(
        dispatch_kernel,
        out_shape=slots,
        in_specs=[pl.BlockSpec(memory_space=pltpu.HBM)] * 2,
        out_specs=pl.BlockSpec(memory_space=pltpu.VMEM),
        scratch_shapes=[
            pltpu.VMEM(ids_t.shape, jnp.int32),
            pltpu.VMEM((lanes, wide), BF16),
            pltpu.SemaphoreType.DMA((PARTS + 1,)),
        ],
        compiler_params=pltpu.CompilerParams(vmem_limit_bytes=16 << 20),
        cost_estimate=pl.CostEstimate(flops=20_000_000_000, bytes_accessed=100_000_000, transcendentals=0),
        name="dispatch",
    )(pltpu.with_memory_space_constraint(ids_t, pltpu.HBM), pltpu.with_memory_space_constraint(tokens, pltpu.HBM))
    finished, weights = pl.pallas_call(
        expert_kernel,
        out_shape=[slots, jax.ShapeDtypeStruct((3 * lanes, piece_rows), BF16)],
        in_specs=vmem(6),
        out_specs=vmem(2),
        scratch_shapes=[
            pltpu.VMEM((experts * CAP, features), BF16),
            pltpu.VMEM((experts * CAP, units), BF16),
        ],
        compiler_params=pltpu.CompilerParams(vmem_limit_bytes=16 << 20),
        cost_estimate=pl.CostEstimate(flops=6_500_000_000, bytes_accessed=30_000_000, transcendentals=0),
        name="expert",
    )(ids_t, gates_t, exchange(outgoing), w_gate[0], w_up[0], w_down[0])
    return pl.pallas_call(
        combine_kernel,
        out_shape=jax.ShapeDtypeStruct((toks, features), BF16),
        in_specs=vmem(2),
        out_specs=pl.BlockSpec(memory_space=pltpu.VMEM),
        compiler_params=pltpu.CompilerParams(vmem_limit_bytes=16 << 20),
        name="combine",
    )(weights, exchange(finished))


def solution(mesh):
    rows = P(("node", "local"), None)
    block = P(("node", "local"), None, None)
    return jax.shard_map(
        on_device,
        mesh=mesh,
        in_specs=(rows, rows, rows, block, block, block),
        out_specs=rows,
        check_vma=False,
    )
```

```python
import functools

import jax
import jax.numpy as jnp
from jax import lax
from jax.experimental import pallas as pl
from jax.experimental.pallas import tpu as pltpu
from jax.sharding import PartitionSpec as P

CAP = 2
PARTS = 4
ROWS = CAP * PARTS
BF16 = jnp.bfloat16
F32 = jnp.float32


def vmem(count):
    return [pl.BlockSpec(memory_space=pltpu.VMEM)] * count


def columns(wide_t):
    top, toks = wide_t.shape
    return jnp.concatenate([wide_t] * (128 // toks), axis=1).T[:toks]


def routing(ids_t, values_t, experts):
    top, toks = ids_t.shape
    shape = (toks, experts * ROWS)
    row = lax.broadcasted_iota(jnp.int32, shape, 1)
    ids = columns(ids_t)
    expert = row // ROWS
    named = [expert == ids[:, k : k + 1] for k in range(top)]
    member = functools.reduce(jnp.logical_or, named).astype(F32)
    later = lax.broadcasted_iota(jnp.int32, (toks, toks), 0)
    sooner = lax.broadcasted_iota(jnp.int32, (toks, toks), 1)
    earlier = (sooner < later).astype(F32).astype(BF16)
    before = jnp.dot(earlier, member.astype(BF16), preferred_element_type=F32)
    own = before == (row % CAP).astype(F32)
    if values_t is not None:
        values = columns(values_t)
        member = jnp.zeros(shape, F32)
        for k, here in enumerate(named):
            member = jnp.where(here, values[:, k : k + 1], member)
    return jnp.where(own, member, 0.0)


def by_part(filled):
    part_of = (lax.broadcasted_iota(jnp.int32, filled.shape, 1) % ROWS) // CAP
    return jnp.concatenate([jnp.where(part_of == part, filled, 0.0) for part in range(PARTS)], axis=0).astype(BF16)


def dispatch_kernel(ids_hbm, tok_hbm, out_ref, ids_ref, tok_parts, sems):
    toks = tok_hbm.shape[0]
    wide = tok_parts.shape[1]
    experts = out_ref.shape[0] // ROWS
    ids_load = pltpu.make_async_copy(ids_hbm, ids_ref, sems.at[PARTS])
    ids_load.start()
    loads = []
    for part in range(PARTS):
        source = tok_hbm.at[:, pl.ds(part * wide, wide)]
        loads.append(pltpu.make_async_copy(source, tok_parts.at[pl.ds(part * toks, toks), :], sems.at[part]))
        loads[-1].start()
    ids_load.wait()
    select = by_part(routing(ids_ref[...], None, experts))
    for load in loads:
        load.wait()
    out_ref[...] = lax.dot_general(
        select, tok_parts[...], (((0,), (0,)), ((), ())), preferred_element_type=F32
    ).astype(BF16)


def combine_weights(ids_t, gates_t, out_ref):
    lanes = out_ref.shape[0] // 3
    rest = routing(ids_t, gates_t, out_ref.shape[1] // ROWS)
    for term in range(3):
        piece = rest.astype(BF16).astype(F32)
        out_ref[term * lanes : (term + 1) * lanes, :] = by_part(piece)
        rest = rest - piece


def combine_kernel(weights_ref, rows_ref, out_ref):
    toks = out_ref.shape[0]
    wide = rows_ref.shape[1]
    lanes = weights_ref.shape[0] // 3
    terms = jnp.dot(weights_ref[...], rows_ref[...], preferred_element_type=F32)
    total = terms[:lanes] + terms[lanes : 2 * lanes] + terms[2 * lanes :]
    for part in range(PARTS):
        out_ref[:, part * wide : (part + 1) * wide] = total[part * toks : (part + 1) * toks].astype(BF16)


def expert_kernel(ids_ref, gates_ref, rows_ref, gate_ref, up_ref, down_ref, out_ref, weights_ref, x, hidden):
    wide = rows_ref.shape[1]
    units = gate_ref.shape[1]
    chunk = 256
    pieces = chunk // ROWS
    here = pieces * CAP
    blocks = range(rows_ref.shape[0] // chunk)

    def parts_of(block):
        return rows_ref[block * chunk : (block + 1) * chunk, :].reshape(pieces, ROWS, wide)

    def gather(part, which):
        for b in which:
            rows = parts_of(b)[:, part * CAP : (part + 1) * CAP, :].reshape(here, wide)
            x[b * here : (b + 1) * here, part * wide : (part + 1) * wide] = rows

    def activate(cols, g, u):
        hidden[:, cols] = (g / (1.0 + jnp.exp(-g)) * u).astype(BF16)

    gather(0, blocks)
    cols = slice(0, chunk)
    g = u = None
    for part in range(PARTS):
        depth = slice(part * wide, (part + 1) * wide)
        gate_term = jnp.dot(x[:, depth], gate_ref[depth, cols], preferred_element_type=F32)
        if part + 1 < PARTS:
            gather(part + 1, blocks[: len(blocks) // 2])
        up_term = jnp.dot(x[:, depth], up_ref[depth, cols], preferred_element_type=F32)
        if part + 1 < PARTS:
            gather(part + 1, blocks[len(blocks) // 2 :])
        g = gate_term if g is None else g + gate_term
        u = up_term if u is None else u + up_term
    activate(cols, g, u)
    for i in range(1, units // chunk):
        cols = slice(i * chunk, (i + 1) * chunk)
        g = jnp.dot(x[...], gate_ref[:, cols], preferred_element_type=F32)
        u = jnp.dot(x[...], up_ref[:, cols], preferred_element_type=F32)
        activate(cols, g, u)
    combine_weights(ids_ref[...], gates_ref[...], weights_ref)
    for part in range(PARTS):
        cols = slice(part * wide, (part + 1) * wide)
        x[:, cols] = jnp.dot(hidden[...], down_ref[:, cols], preferred_element_type=F32).astype(BF16)
    first = lax.broadcasted_iota(jnp.int32, (chunk, chunk), 0)
    second = lax.broadcasted_iota(jnp.int32, (chunk, chunk), 1)
    source = ((first % ROWS) // CAP) * here + (first // ROWS) * CAP + first % CAP
    group = (second == source).astype(F32).astype(BF16)
    for b in blocks:
        own = [x[b * here : (b + 1) * here, part * wide : (part + 1) * wide] for part in range(PARTS)]
        out_ref[b * chunk : (b + 1) * chunk, :] = jnp.dot(
            group, jnp.concatenate(own, axis=0), preferred_element_type=F32
        ).astype(BF16)


def on_device(tokens, expert_ids, gate_values, w_gate, w_up, w_down):
    experts = lax.axis_size("node") * lax.axis_size("local")
    toks, features = tokens.shape
    units = w_gate.shape[2]
    wide = features // PARTS
    lanes = PARTS * toks
    piece_rows = experts * ROWS
    ids_t, gates_t = expert_ids.T, gate_values.T
    slots = jax.ShapeDtypeStruct((piece_rows, wide), BF16)

    def exchange(rows):
        moved = lax.all_to_all(
            rows.reshape(experts, ROWS, wide), ("node", "local"), split_axis=0, concat_axis=0, tiled=True
        )
        return moved.reshape(piece_rows, wide)

    outgoing = pl.pallas_call(
        dispatch_kernel,
        out_shape=slots,
        in_specs=[pl.BlockSpec(memory_space=pltpu.HBM)] * 2,
        out_specs=pl.BlockSpec(memory_space=pltpu.VMEM),
        scratch_shapes=[
            pltpu.VMEM(ids_t.shape, jnp.int32),
            pltpu.VMEM((lanes, wide), BF16),
            pltpu.SemaphoreType.DMA((PARTS + 1,)),
        ],
        compiler_params=pltpu.CompilerParams(vmem_limit_bytes=16 << 20),
        cost_estimate=pl.CostEstimate(flops=20_000_000_000, bytes_accessed=100_000_000, transcendentals=0),
        name="dispatch",
    )(pltpu.with_memory_space_constraint(ids_t, pltpu.HBM), pltpu.with_memory_space_constraint(tokens, pltpu.HBM))
    finished, weights = pl.pallas_call(
        expert_kernel,
        out_shape=[slots, jax.ShapeDtypeStruct((3 * lanes, piece_rows), BF16)],
        in_specs=vmem(6),
        out_specs=vmem(2),
        scratch_shapes=[
            pltpu.VMEM((experts * CAP, features), BF16),
            pltpu.VMEM((experts * CAP, units), BF16),
        ],
        compiler_params=pltpu.CompilerParams(vmem_limit_bytes=16 << 20),
        cost_estimate=pl.CostEstimate(flops=6_500_000_000, bytes_accessed=30_000_000, transcendentals=0),
        name="expert",
    )(ids_t, gates_t, exchange(outgoing), w_gate[0], w_up[0], w_down[0])
    return pl.pallas_call(
        combine_kernel,
        out_shape=jax.ShapeDtypeStruct((toks, features), BF16),
        in_specs=vmem(2),
        out_specs=pl.BlockSpec(memory_space=pltpu.VMEM),
        compiler_params=pltpu.CompilerParams(vmem_limit_bytes=16 << 20),
        name="combine",
    )(weights, exchange(finished))


def solution(mesh):
    rows = P(("node", "local"), None)
    block = P(("node", "local"), None, None)
    return jax.shard_map(
        on_device,
        mesh=mesh,
        in_specs=(rows, rows, rows, block, block, block),
        out_specs=rows,
        check_vma=False,
    )
```

```python
import functools

import jax
import jax.numpy as jnp
from jax import lax
from jax.experimental import pallas as pl
from jax.experimental.pallas import tpu as pltpu
from jax.sharding import PartitionSpec as P

CAP = 2
PARTS = 4
ROWS = CAP * PARTS
BF16 = jnp.bfloat16
F32 = jnp.float32


def vmem(count):
    return [pl.BlockSpec(memory_space=pltpu.VMEM)] * count


def columns(wide_t):
    top, toks = wide_t.shape
    return jnp.concatenate([wide_t] * (128 // toks), axis=1).T[:toks]


def named_rows(ids_t, rows):
    top, toks = ids_t.shape
    expert = lax.broadcasted_iota(jnp.int32, (toks, rows), 1) // ROWS
    ids = columns(ids_t)
    return [expert == ids[:, k : k + 1] for k in range(top)]


def routing(ids_t, experts):
    toks = ids_t.shape[1]
    member = functools.reduce(jnp.logical_or, named_rows(ids_t, experts * ROWS)).astype(F32)
    later = lax.broadcasted_iota(jnp.int32, (toks, toks), 0)
    sooner = lax.broadcasted_iota(jnp.int32, (toks, toks), 1)
    earlier = (sooner < later).astype(F32).astype(BF16)
    before = jnp.dot(earlier, member.astype(BF16), preferred_element_type=F32)
    row = lax.broadcasted_iota(jnp.int32, member.shape, 1)
    own = before == ((row // PARTS) % CAP).astype(F32)
    return jnp.where(own, member, 0.0)


def by_part(filled):
    part_of = lax.broadcasted_iota(jnp.int32, filled.shape, 1) % PARTS
    return jnp.concatenate([jnp.where(part_of == part, filled, 0.0) for part in range(PARTS)], axis=0).astype(BF16)


def dispatch_kernel(ids_hbm, tok_hbm, out_ref, filled_ref, ids_ref, tok_parts, sems):
    toks = tok_hbm.shape[0]
    wide = tok_parts.shape[1]
    experts = out_ref.shape[0] // ROWS
    ids_load = pltpu.make_async_copy(ids_hbm, ids_ref, sems.at[PARTS])
    ids_load.start()
    loads = []
    for part in range(PARTS):
        source = tok_hbm.at[:, pl.ds(part * wide, wide)]
        loads.append(pltpu.make_async_copy(source, tok_parts.at[pl.ds(part * toks, toks), :], sems.at[part]))
        loads[-1].start()
    ids_load.wait()
    filled = routing(ids_ref[...], experts)
    filled_ref[...] = filled.astype(BF16)
    select = by_part(filled)
    for load in loads:
        load.wait()
    out_ref[...] = lax.dot_general(
        select, tok_parts[...], (((0,), (0,)), ((), ())), preferred_element_type=F32
    ).astype(BF16)


def combine_weights(ids_t, gates_t, filled, out_ref):
    lanes = out_ref.shape[0] // 3
    gates = columns(gates_t)
    rest = jnp.zeros(filled.shape, F32)
    for k, here in enumerate(named_rows(ids_t, filled.shape[1])):
        rest = jnp.where(here, gates[:, k : k + 1], rest)
    rest = rest * filled.astype(F32)
    for term in range(3):
        piece = rest.astype(BF16).astype(F32)
        out_ref[term * lanes : (term + 1) * lanes, :] = by_part(piece)
        rest = rest - piece


def combine_kernel(weights_ref, rows_ref, out_ref):
    toks = out_ref.shape[0]
    wide = rows_ref.shape[1]
    lanes = weights_ref.shape[0] // 3
    terms = jnp.dot(weights_ref[...], rows_ref[...], preferred_element_type=F32)
    total = terms[:lanes] + terms[lanes : 2 * lanes] + terms[2 * lanes :]
    for part in range(PARTS):
        out_ref[:, part * wide : (part + 1) * wide] = total[part * toks : (part + 1) * toks].astype(BF16)


def expert_kernel(ids_ref, gates_ref, filled_ref, rows_ref, gate_ref, up_ref, down_ref, out_ref, weights_ref, x, hidden):
    wide = rows_ref.shape[1]
    units = gate_ref.shape[1]
    count = x.shape[0]
    chunk = 256
    pieces = 256 // ROWS
    first = lax.broadcasted_iota(jnp.int32, (256, 256), 0)
    second = lax.broadcasted_iota(jnp.int32, (256, 256), 1)
    ungroup = (second == (first % pieces) * ROWS + first // pieces).astype(F32).astype(BF16)
    group = (first == (second % pieces) * ROWS + second // pieces).astype(F32).astype(BF16)
    half = count // CAP
    for b in range(rows_ref.shape[0] // 256):
        spread = jnp.dot(ungroup, rows_ref[b * 256 : (b + 1) * 256, :], preferred_element_type=F32).astype(BF16)
        for r in range(ROWS):
            slot, part = r // PARTS, r % PARTS
            start = slot * half + b * pieces
            x[start : start + pieces, part * wide : (part + 1) * wide] = spread[r * pieces : (r + 1) * pieces]
    for i in range(units // chunk):
        cols = slice(i * chunk, (i + 1) * chunk)
        g = jnp.dot(x[...], gate_ref[:, cols], preferred_element_type=F32)
        u = jnp.dot(x[...], up_ref[:, cols], preferred_element_type=F32)
        hidden[:, cols] = (g / (1.0 + jnp.exp(-g)) * u).astype(BF16)
        if i == 0:
            combine_weights(ids_ref[...], gates_ref[...], filled_ref[...], weights_ref)
    for part in range(PARTS):
        cols = slice(part * wide, (part + 1) * wide)
        x[:, cols] = jnp.dot(hidden[...], down_ref[:, cols], preferred_element_type=F32).astype(BF16)
    for b in range(rows_ref.shape[0] // 256):
        parts = []
        for r in range(ROWS):
            slot, part = r // PARTS, r % PARTS
            start = slot * half + b * pieces
            parts.append(x[start : start + pieces, part * wide : (part + 1) * wide])
        out_ref[b * 256 : (b + 1) * 256, :] = jnp.dot(
            group, jnp.concatenate(parts, axis=0), preferred_element_type=F32
        ).astype(BF16)


def on_device(tokens, expert_ids, gate_values, w_gate, w_up, w_down):
    experts = lax.axis_size("node") * lax.axis_size("local")
    toks, features = tokens.shape
    units = w_gate.shape[2]
    wide = features // PARTS
    lanes = PARTS * toks
    piece_rows = experts * ROWS
    ids_t, gates_t = expert_ids.T, gate_values.T
    slots = jax.ShapeDtypeStruct((piece_rows, wide), BF16)

    def exchange(rows):
        moved = lax.all_to_all(
            rows.reshape(experts, ROWS, wide), ("node", "local"), split_axis=0, concat_axis=0, tiled=True
        )
        return moved.reshape(piece_rows, wide)

    outgoing, filled = pl.pallas_call(
        dispatch_kernel,
        out_shape=[slots, jax.ShapeDtypeStruct((toks, piece_rows), BF16)],
        in_specs=[pl.BlockSpec(memory_space=pltpu.HBM)] * 2,
        out_specs=vmem(2),
        scratch_shapes=[
            pltpu.VMEM(ids_t.shape, jnp.int32),
            pltpu.VMEM((lanes, wide), BF16),
            pltpu.SemaphoreType.DMA((PARTS + 1,)),
        ],
        compiler_params=pltpu.CompilerParams(vmem_limit_bytes=16 << 20),
        cost_estimate=pl.CostEstimate(flops=20_000_000_000, bytes_accessed=100_000_000, transcendentals=0),
        name="dispatch",
    )(pltpu.with_memory_space_constraint(ids_t, pltpu.HBM), pltpu.with_memory_space_constraint(tokens, pltpu.HBM))
    finished, weights = pl.pallas_call(
        expert_kernel,
        out_shape=[slots, jax.ShapeDtypeStruct((3 * lanes, piece_rows), BF16)],
        in_specs=vmem(7),
        out_specs=vmem(2),
        scratch_shapes=[
            pltpu.VMEM((experts * CAP, features), BF16),
            pltpu.VMEM((experts * CAP, units), BF16),
        ],
        compiler_params=pltpu.CompilerParams(vmem_limit_bytes=16 << 20),
        cost_estimate=pl.CostEstimate(flops=6_500_000_000, bytes_accessed=30_000_000, transcendentals=0),
        name="expert",
    )(ids_t, gates_t, filled, exchange(outgoing), w_gate[0], w_up[0], w_down[0])
    return pl.pallas_call(
        combine_kernel,
        out_shape=jax.ShapeDtypeStruct((toks, features), BF16),
        in_specs=vmem(2),
        out_specs=pl.BlockSpec(memory_space=pltpu.VMEM),
        compiler_params=pltpu.CompilerParams(vmem_limit_bytes=16 << 20),
        name="combine",
    )(weights, exchange(finished))


def solution(mesh):
    rows = P(("node", "local"), None)
    block = P(("node", "local"), None, None)
    return jax.shard_map(
        on_device,
        mesh=mesh,
        in_specs=(rows, rows, rows, block, block, block),
        out_specs=rows,
        check_vma=False,
    )
```

```python
import functools

import jax
import jax.numpy as jnp
from jax import lax
from jax.experimental import pallas as pl
from jax.experimental.pallas import tpu as pltpu
from jax.sharding import PartitionSpec as P

CAP = 2
PARTS = 4
ROWS = CAP * PARTS
BF16 = jnp.bfloat16
F32 = jnp.float32


def vmem(count):
    return [pl.BlockSpec(memory_space=pltpu.VMEM)] * count


def columns(wide_t):
    top, toks = wide_t.shape
    return jnp.concatenate([wide_t] * (128 // toks), axis=1).T[:toks]


def named_rows(ids_t, rows):
    top, toks = ids_t.shape
    expert = lax.broadcasted_iota(jnp.int32, (toks, rows), 1) // ROWS
    ids = columns(ids_t)
    return [expert == ids[:, k : k + 1] for k in range(top)]


def routing(ids_t, experts):
    toks = ids_t.shape[1]
    member = functools.reduce(jnp.logical_or, named_rows(ids_t, experts * ROWS)).astype(F32)
    later = lax.broadcasted_iota(jnp.int32, (toks, toks), 0)
    sooner = lax.broadcasted_iota(jnp.int32, (toks, toks), 1)
    earlier = (sooner < later).astype(F32).astype(BF16)
    before = jnp.dot(earlier, member.astype(BF16), preferred_element_type=F32)
    row = lax.broadcasted_iota(jnp.int32, member.shape, 1)
    own = before == (row % CAP).astype(F32)
    return jnp.where(own, member, 0.0)


def by_part(filled):
    part_of = (lax.broadcasted_iota(jnp.int32, filled.shape, 1) % ROWS) // CAP
    return jnp.concatenate([jnp.where(part_of == part, filled, 0.0) for part in range(PARTS)], axis=0).astype(BF16)


def dispatch_kernel(ids_hbm, tok_hbm, out_ref, filled_ref, ids_ref, tok_parts, sems):
    toks = tok_hbm.shape[0]
    wide = tok_parts.shape[1]
    experts = out_ref.shape[0] // ROWS
    ids_load = pltpu.make_async_copy(ids_hbm, ids_ref, sems.at[PARTS])
    ids_load.start()
    loads = []
    for part in range(PARTS):
        source = tok_hbm.at[:, pl.ds(part * wide, wide)]
        loads.append(pltpu.make_async_copy(source, tok_parts.at[pl.ds(part * toks, toks), :], sems.at[part]))
        loads[-1].start()
    ids_load.wait()
    filled = routing(ids_ref[...], experts)
    filled_ref[...] = filled.astype(BF16)
    select = by_part(filled)
    for load in loads:
        load.wait()
    out_ref[...] = lax.dot_general(
        select, tok_parts[...], (((0,), (0,)), ((), ())), preferred_element_type=F32
    ).astype(BF16)


def combine_weights(ids_t, gates_t, filled, out_ref):
    lanes = out_ref.shape[0] // 3
    gates = columns(gates_t)
    rest = jnp.zeros(filled.shape, F32)
    for k, here in enumerate(named_rows(ids_t, filled.shape[1])):
        rest = jnp.where(here, gates[:, k : k + 1], rest)
    rest = rest * filled.astype(F32)
    for term in range(3):
        piece = rest.astype(BF16).astype(F32)
        out_ref[term * lanes : (term + 1) * lanes, :] = by_part(piece)
        rest = rest - piece


def combine_kernel(weights_ref, rows_ref, out_ref):
    toks = out_ref.shape[0]
    wide = rows_ref.shape[1]
    lanes = weights_ref.shape[0] // 3
    terms = jnp.dot(weights_ref[...], rows_ref[...], preferred_element_type=F32)
    total = terms[:lanes] + terms[lanes : 2 * lanes] + terms[2 * lanes :]
    for part in range(PARTS):
        out_ref[:, part * wide : (part + 1) * wide] = total[part * toks : (part + 1) * toks].astype(BF16)


def expert_kernel(ids_ref, gates_ref, filled_ref, rows_ref, gate_ref, up_ref, down_ref, out_ref, weights_ref, x, hidden):
    wide = rows_ref.shape[1]
    units = gate_ref.shape[1]
    chunk = 256
    pieces = chunk // ROWS
    here = pieces * CAP
    blocks = range(rows_ref.shape[0] // chunk)

    def parts_of(block):
        return rows_ref[block * chunk : (block + 1) * chunk, :].reshape(pieces, ROWS, wide)

    def gather(part, which):
        for b in which:
            rows = parts_of(b)[:, part * CAP : (part + 1) * CAP, :].reshape(here, wide)
            x[b * here : (b + 1) * here, part * wide : (part + 1) * wide] = rows

    def activate(cols, g, u):
        hidden[:, cols] = (g / (1.0 + jnp.exp(-g)) * u).astype(BF16)

    gather(0, blocks)
    cols = slice(0, chunk)
    g = u = None
    for part in range(PARTS):
        depth = slice(part * wide, (part + 1) * wide)
        gate_term = jnp.dot(x[:, depth], gate_ref[depth, cols], preferred_element_type=F32)
        if part + 1 < PARTS:
            gather(part + 1, blocks[: len(blocks) // 2])
        up_term = jnp.dot(x[:, depth], up_ref[depth, cols], preferred_element_type=F32)
        if part + 1 < PARTS:
            gather(part + 1, blocks[len(blocks) // 2 :])
        g = gate_term if g is None else g + gate_term
        u = up_term if u is None else u + up_term
    activate(cols, g, u)
    for i in range(1, units // chunk):
        cols = slice(i * chunk, (i + 1) * chunk)
        g = jnp.dot(x[...], gate_ref[:, cols], preferred_element_type=F32)
        u = jnp.dot(x[...], up_ref[:, cols], preferred_element_type=F32)
        activate(cols, g, u)
    combine_weights(ids_ref[...], gates_ref[...], filled_ref[...], weights_ref)
    for part in range(PARTS):
        cols = slice(part * wide, (part + 1) * wide)
        x[:, cols] = jnp.dot(hidden[...], down_ref[:, cols], preferred_element_type=F32).astype(BF16)
    first = lax.broadcasted_iota(jnp.int32, (chunk, chunk), 0)
    second = lax.broadcasted_iota(jnp.int32, (chunk, chunk), 1)
    source = ((first % ROWS) // CAP) * here + (first // ROWS) * CAP + first % CAP
    group = (second == source).astype(F32).astype(BF16)
    for b in blocks:
        own = [x[b * here : (b + 1) * here, part * wide : (part + 1) * wide] for part in range(PARTS)]
        out_ref[b * chunk : (b + 1) * chunk, :] = jnp.dot(
            group, jnp.concatenate(own, axis=0), preferred_element_type=F32
        ).astype(BF16)


def on_device(tokens, expert_ids, gate_values, w_gate, w_up, w_down):
    experts = lax.axis_size("node") * lax.axis_size("local")
    toks, features = tokens.shape
    units = w_gate.shape[2]
    wide = features // PARTS
    lanes = PARTS * toks
    piece_rows = experts * ROWS
    ids_t, gates_t = expert_ids.T, gate_values.T
    slots = jax.ShapeDtypeStruct((piece_rows, wide), BF16)

    def exchange(rows):
        moved = lax.all_to_all(
            rows.reshape(experts, ROWS, wide), ("node", "local"), split_axis=0, concat_axis=0, tiled=True
        )
        return moved.reshape(piece_rows, wide)

    outgoing, filled = pl.pallas_call(
        dispatch_kernel,
        out_shape=[slots, jax.ShapeDtypeStruct((toks, piece_rows), BF16)],
        in_specs=[pl.BlockSpec(memory_space=pltpu.HBM)] * 2,
        out_specs=vmem(2),
        scratch_shapes=[
            pltpu.VMEM(ids_t.shape, jnp.int32),
            pltpu.VMEM((lanes, wide), BF16),
            pltpu.SemaphoreType.DMA((PARTS + 1,)),
        ],
        compiler_params=pltpu.CompilerParams(vmem_limit_bytes=16 << 20),
        cost_estimate=pl.CostEstimate(flops=20_000_000_000, bytes_accessed=100_000_000, transcendentals=0),
        name="dispatch",
    )(pltpu.with_memory_space_constraint(ids_t, pltpu.HBM), pltpu.with_memory_space_constraint(tokens, pltpu.HBM))
    finished, weights = pl.pallas_call(
        expert_kernel,
        out_shape=[slots, jax.ShapeDtypeStruct((3 * lanes, piece_rows), BF16)],
        in_specs=vmem(7),
        out_specs=vmem(2),
        scratch_shapes=[
            pltpu.VMEM((experts * CAP, features), BF16),
            pltpu.VMEM((experts * CAP, units), BF16),
        ],
        compiler_params=pltpu.CompilerParams(vmem_limit_bytes=16 << 20),
        cost_estimate=pl.CostEstimate(flops=6_500_000_000, bytes_accessed=30_000_000, transcendentals=0),
        name="expert",
    )(ids_t, gates_t, filled, exchange(outgoing), w_gate[0], w_up[0], w_down[0])
    return pl.pallas_call(
        combine_kernel,
        out_shape=jax.ShapeDtypeStruct((toks, features), BF16),
        in_specs=vmem(2),
        out_specs=pl.BlockSpec(memory_space=pltpu.VMEM),
        compiler_params=pltpu.CompilerParams(vmem_limit_bytes=16 << 20),
        name="combine",
    )(weights, exchange(finished))


def solution(mesh):
    rows = P(("node", "local"), None)
    block = P(("node", "local"), None, None)
    return jax.shard_map(
        on_device,
        mesh=mesh,
        in_specs=(rows, rows, rows, block, block, block),
        out_specs=rows,
        check_vma=False,
    )
```

```python
import functools

import jax
import jax.numpy as jnp
from jax import lax
from jax.experimental import pallas as pl
from jax.experimental.pallas import tpu as pltpu
from jax.sharding import PartitionSpec as P

CAP = 2
PARTS = 4
ROWS = CAP * PARTS
BF16 = jnp.bfloat16
F32 = jnp.float32


def vmem(count):
    return [pl.BlockSpec(memory_space=pltpu.VMEM)] * count


def columns(wide_t):
    top, toks = wide_t.shape
    return jnp.concatenate([wide_t] * (128 // toks), axis=1).T[:toks]


def named_rows(ids_t, rows):
    top, toks = ids_t.shape
    expert = lax.broadcasted_iota(jnp.int32, (toks, rows), 1) // ROWS
    ids = columns(ids_t)
    return [expert == ids[:, k : k + 1] for k in range(top)]


def routing(ids_t, experts):
    toks = ids_t.shape[1]
    member = functools.reduce(jnp.logical_or, named_rows(ids_t, experts * ROWS)).astype(F32)
    later = lax.broadcasted_iota(jnp.int32, (toks, toks), 0)
    sooner = lax.broadcasted_iota(jnp.int32, (toks, toks), 1)
    earlier = (sooner < later).astype(F32).astype(BF16)
    before = jnp.dot(earlier, member.astype(BF16), preferred_element_type=F32)
    row = lax.broadcasted_iota(jnp.int32, member.shape, 1)
    own = before == (row % CAP).astype(F32)
    return jnp.where(own, member, 0.0)


def by_part(filled):
    part_of = (lax.broadcasted_iota(jnp.int32, filled.shape, 1) % ROWS) // CAP
    return jnp.concatenate([jnp.where(part_of == part, filled, 0.0) for part in range(PARTS)], axis=0).astype(BF16)


def dispatch_kernel(ids_hbm, tok_hbm, out_ref, filled_ref, ids_ref, tok_parts, sems):
    toks = tok_hbm.shape[0]
    wide = tok_parts.shape[1]
    experts = out_ref.shape[0] // ROWS
    ids_load = pltpu.make_async_copy(ids_hbm, ids_ref, sems.at[PARTS])
    ids_load.start(priority=1)
    loads = []
    for part in range(PARTS):
        source = tok_hbm.at[:, pl.ds(part * wide, wide)]
        loads.append(pltpu.make_async_copy(source, tok_parts.at[pl.ds(part * toks, toks), :], sems.at[part]))
        loads[-1].start(priority=1)
    ids_load.wait()
    filled = routing(ids_ref[...], experts)
    filled_ref[...] = filled.astype(BF16)
    select = by_part(filled)
    for load in loads:
        load.wait()
    out_ref[...] = lax.dot_general(
        select, tok_parts[...], (((0,), (0,)), ((), ())), preferred_element_type=F32
    ).astype(BF16)


def combine_weights(ids_t, gates_t, filled, out_ref):
    lanes = out_ref.shape[0] // 3
    gates = columns(gates_t)
    rest = jnp.zeros(filled.shape, F32)
    for k, here in enumerate(named_rows(ids_t, filled.shape[1])):
        rest = jnp.where(here, gates[:, k : k + 1], rest)
    rest = rest * filled.astype(F32)
    for term in range(3):
        piece = rest.astype(BF16).astype(F32)
        out_ref[term * lanes : (term + 1) * lanes, :] = by_part(piece)
        rest = rest - piece


def combine_kernel(weights_ref, rows_ref, out_ref):
    toks = out_ref.shape[0]
    wide = rows_ref.shape[1]
    lanes = weights_ref.shape[0] // 3
    terms = jnp.dot(weights_ref[...], rows_ref[...], preferred_element_type=F32)
    total = terms[:lanes] + terms[lanes : 2 * lanes] + terms[2 * lanes :]
    for part in range(PARTS):
        out_ref[:, part * wide : (part + 1) * wide] = total[part * toks : (part + 1) * toks].astype(BF16)


def expert_kernel(ids_ref, gates_ref, filled_ref, rows_ref, gate_ref, up_ref, down_ref, out_ref, weights_ref, x, hidden):
    wide = rows_ref.shape[1]
    units = gate_ref.shape[1]
    chunk = 256
    pieces = chunk // ROWS
    here = pieces * CAP
    blocks = range(rows_ref.shape[0] // chunk)

    def parts_of(block):
        return rows_ref[block * chunk : (block + 1) * chunk, :].reshape(pieces, ROWS, wide)

    def gather(part, which):
        for b in which:
            rows = parts_of(b)[:, part * CAP : (part + 1) * CAP, :].reshape(here, wide)
            x[b * here : (b + 1) * here, part * wide : (part + 1) * wide] = rows

    def activate(cols, g, u):
        hidden[:, cols] = (g / (1.0 + jnp.exp(-g)) * u).astype(BF16)

    gather(0, blocks)
    cols = slice(0, chunk)
    g = u = None
    for part in range(PARTS):
        depth = slice(part * wide, (part + 1) * wide)
        gate_term = jnp.dot(x[:, depth], gate_ref[depth, cols], preferred_element_type=F32)
        if part + 1 < PARTS:
            gather(part + 1, blocks[: len(blocks) // 2])
        up_term = jnp.dot(x[:, depth], up_ref[depth, cols], preferred_element_type=F32)
        if part + 1 < PARTS:
            gather(part + 1, blocks[len(blocks) // 2 :])
        g = gate_term if g is None else g + gate_term
        u = up_term if u is None else u + up_term
    activate(cols, g, u)
    for i in range(1, units // chunk):
        cols = slice(i * chunk, (i + 1) * chunk)
        g = jnp.dot(x[...], gate_ref[:, cols], preferred_element_type=F32)
        u = jnp.dot(x[...], up_ref[:, cols], preferred_element_type=F32)
        activate(cols, g, u)
    combine_weights(ids_ref[...], gates_ref[...], filled_ref[...], weights_ref)
    for part in range(PARTS):
        cols = slice(part * wide, (part + 1) * wide)
        x[:, cols] = jnp.dot(hidden[...], down_ref[:, cols], preferred_element_type=F32).astype(BF16)
    first = lax.broadcasted_iota(jnp.int32, (chunk, chunk), 0)
    second = lax.broadcasted_iota(jnp.int32, (chunk, chunk), 1)
    source = ((first % ROWS) // CAP) * here + (first // ROWS) * CAP + first % CAP
    group = (second == source).astype(F32).astype(BF16)
    for b in blocks:
        own = [x[b * here : (b + 1) * here, part * wide : (part + 1) * wide] for part in range(PARTS)]
        out_ref[b * chunk : (b + 1) * chunk, :] = jnp.dot(
            group, jnp.concatenate(own, axis=0), preferred_element_type=F32
        ).astype(BF16)


def on_device(tokens, expert_ids, gate_values, w_gate, w_up, w_down):
    experts = lax.axis_size("node") * lax.axis_size("local")
    toks, features = tokens.shape
    units = w_gate.shape[2]
    wide = features // PARTS
    lanes = PARTS * toks
    piece_rows = experts * ROWS
    ids_t, gates_t = expert_ids.T, gate_values.T
    slots = jax.ShapeDtypeStruct((piece_rows, wide), BF16)

    def exchange(rows):
        moved = lax.all_to_all(
            rows.reshape(experts, ROWS, wide), ("node", "local"), split_axis=0, concat_axis=0, tiled=True
        )
        return moved.reshape(piece_rows, wide)

    outgoing, filled = pl.pallas_call(
        dispatch_kernel,
        out_shape=[slots, jax.ShapeDtypeStruct((toks, piece_rows), BF16)],
        in_specs=[pl.BlockSpec(memory_space=pltpu.HBM)] * 2,
        out_specs=vmem(2),
        scratch_shapes=[
            pltpu.VMEM(ids_t.shape, jnp.int32),
            pltpu.VMEM((lanes, wide), BF16),
            pltpu.SemaphoreType.DMA((PARTS + 1,)),
        ],
        compiler_params=pltpu.CompilerParams(vmem_limit_bytes=16 << 20),
        cost_estimate=pl.CostEstimate(flops=20_000_000_000, bytes_accessed=100_000_000, transcendentals=0),
        name="dispatch",
    )(pltpu.with_memory_space_constraint(ids_t, pltpu.HBM), pltpu.with_memory_space_constraint(tokens, pltpu.HBM))
    finished, weights = pl.pallas_call(
        expert_kernel,
        out_shape=[slots, jax.ShapeDtypeStruct((3 * lanes, piece_rows), BF16)],
        in_specs=vmem(7),
        out_specs=vmem(2),
        scratch_shapes=[
            pltpu.VMEM((experts * CAP, features), BF16),
            pltpu.VMEM((experts * CAP, units), BF16),
        ],
        compiler_params=pltpu.CompilerParams(vmem_limit_bytes=16 << 20),
        cost_estimate=pl.CostEstimate(flops=6_500_000_000, bytes_accessed=30_000_000, transcendentals=0),
        name="expert",
    )(ids_t, gates_t, filled, exchange(outgoing), w_gate[0], w_up[0], w_down[0])
    return pl.pallas_call(
        combine_kernel,
        out_shape=jax.ShapeDtypeStruct((toks, features), BF16),
        in_specs=vmem(2),
        out_specs=pl.BlockSpec(memory_space=pltpu.VMEM),
        compiler_params=pltpu.CompilerParams(vmem_limit_bytes=16 << 20),
        name="combine",
    )(weights, exchange(finished))


def solution(mesh):
    rows = P(("node", "local"), None)
    block = P(("node", "local"), None, None)
    return jax.shard_map(
        on_device,
        mesh=mesh,
        in_specs=(rows, rows, rows, block, block, block),
        out_specs=rows,
        check_vma=False,
    )
```
